128 devices in a mesh: row: 16 (over z, x_lo, core), seq: 8 (over y, x_hi).
Axes of the slice: x: 4 (x_hi: 2, x_lo: 2; x = x_hi * 2 + x_lo), y: 4, z: 4, core: 2. Of those that a mesh axis runs over, the one named last changes fastest.
Arguments:
- tokens_in: bfloat16 [16, 1024, 1024], P('row', 'seq'), may hold values from -6 to 6
- norm_gain: bfloat16 [1024], P(('row', 'seq')), may hold values from 0.5 to 1.5
- w_query: bfloat16 [1024, 1024], P(('row', 'seq')), may hold values from -0.1875 to 0.1875
- w_key: bfloat16 [1024, 512], P(('row', 'seq')), may hold values from -0.1875 to 0.1875
- w_value: bfloat16 [1024, 512], P(('row', 'seq')), may hold values from -0.1875 to 0.1875
- qk_gain: bfloat16 [128], P(('row', 'seq')), may hold values from 0.5 to 1.5
- w_out: bfloat16 [1024, 1024], P(('row', 'seq')), may hold values from -0.75 to 0.75
- moe_gain: bfloat16 [1024], P(('row', 'seq')), may hold values from 0.5 to 1.5
- w_router: bfloat16 [1024, 32], P(('row', 'seq')), may hold values from -0.09375 to 0.09375
- w_gate: bfloat16 [32, 1024, 512], P('row', 'seq'), may hold values from -0.1875 to 0.1875
- w_up: bfloat16 [32, 1024, 512], P('row', 'seq'), may hold values from -0.1875 to 0.1875
- w_down: bfloat16 [32, 512, 1024], P('row', 'seq'), may hold values from -0.75 to 0.75
- segment_ids: int32 [16, 1024], P('row', 'seq'), may hold values from 0 to 2, as said below
- expert_ids: int32 [16, 1024, 8], P('row', 'seq'), may hold values from 0 to 31, all different within a row; in each aligned block of 128 rows (0 to 127, 128 to 255, ..., all dimensions but the last counted through in order) at most 48 rows name the same one
- out_grad: bfloat16 [16, 1024, 1024], P('row', 'seq'), may hold values from -6 to 6
Outputs:
- layer_out: bfloat16 [16, 1024, 1024], P('row', 'seq')
- tokens_grad: bfloat16 [16, 1024, 1024], P('row', 'seq')
- norm_gain_grad: float32 [1024], P(('row', 'seq'))
- w_query_grad: float32 [1024, 1024], P(('row', 'seq'))
- w_key_grad: float32 [1024, 512], P(('row', 'seq'))
- w_value_grad: float32 [1024, 512], P(('row', 'seq'))
- qk_gain_grad: float32 [128], P(('row', 'seq'))
- w_out_grad: float32 [1024, 1024], P(('row', 'seq'))
- moe_gain_grad: float32 [1024], P(('row', 'seq'))
- w_router_grad: float32 [1024, 32], P(('row', 'seq'))
- w_gate_grad: float32 [32, 1024, 512], P('row', 'seq')
- w_up_grad: float32 [32, 1024, 512], P('row', 'seq')
- w_down_grad: float32 [32, 512, 1024], P('row', 'seq')
The draws below stay inside these ranges and needn't reach their ends.
Inputs may be any that keep to these rules, and one draw needn't show every extreme that they name: `segment_ids`: within each row the numbers never fall; tokens with one number form one document. `expert_ids`: A token names 8 different experts. In each aligned block of 128 tokens of a row (the tokens of one device), no expert is named by more than 48 tokens, a bound that some block reaches.
All inputs are finite; a program needn't handle non-finite values.
Results may differ from the reference program's by a relative error of at most 0.035.
Values may be sent and summed in bfloat16 or wider, within the bound.
A program may use at most 128 MiB of HBM per device.

```python
import math
import jax
import jax.numpy as jnp
import numpy as np
from jax import lax

D = 1024
HEADS = 16
KV = 8
HD = 64
FF = 512
TOPK = 8
EXPERTS = 32
LENGTH = 1024
ROWS = 16
S_DEV = 128
CAP = 48
N_SEQ = 8


def draw_segment_ids(key, part):
    key = jax.random.fold_in(key, 11)
    subkeys = jax.random.split(key, 2)
    shortest = max(1, LENGTH * 60 // 1024)
    longest = max(LENGTH * 800 // 1024, LENGTH - 2 * S_DEV + 4)
    first_low = max(shortest, LENGTH - S_DEV + 1 - longest)
    first_cut = jax.random.randint(subkeys[0], (ROWS, 1), first_low, S_DEV)
    second_high = jnp.minimum(first_cut + longest, LENGTH - shortest) + 1
    second_cut = jax.random.randint(subkeys[1], (ROWS, 1), LENGTH - S_DEV + 1, second_high)
    places = jnp.arange(LENGTH, dtype=jnp.int32)[None, :]
    segment = (places >= first_cut).astype(jnp.int32) + (places >= second_cut).astype(jnp.int32)
    return segment


def block_levels(own_key, dims, cuts, low, top_value):
    def one(position, shards_of):
        heights = jax.random.uniform(jax.random.fold_in(jax.random.fold_in(own_key, 6), position), (shards_of,), jnp.float32, low / len(cuts), top_value / len(cuts))
        return jnp.repeat(jnp.exp(heights), dims[position] // shards_of).reshape((-1,) + (1,) * (len(dims) - position - 1))

    loudness = one(*cuts[0])
    for cut in cuts[1:]:
        loudness = loudness * one(*cut)
    return loudness


def deal_out(own_key, own, number, rows, number_of, top, limit, skew):
    order = jax.random.permutation(own_key, number_of)
    heavy_load, common = portions_of(number_of, rows * top, limit, skew, True), portions_of(number_of, rows * top, limit, skew, False)
    places = jnp.arange(number_of)

    def named(tallies, offset_by):
        used = int((tallies > 0).sum())
        fixed = max(1, used // 4)
        moved = fixed + (places - fixed + offset_by * (used - fixed)) % max(1, number_of - fixed)
        return jnp.zeros((number_of,), jnp.int32).at[order[jnp.where(places < fixed, places, moved)]].set(jnp.asarray(tallies, jnp.int32))

    tallies = jnp.where(number % 4 == 0, named(heavy_load, number // 4), named(common, number - number // 4 - 1))
    mixed = jax.random.permutation(jax.random.fold_in(own, 3), number_of)
    source_of, receiver = mixed[0:number_of // 2 * 2:2], mixed[1:number_of // 2 * 2:2]
    slack = jnp.minimum(tallies[source_of] - 1, limit - tallies[receiver]) // 2
    slack = jnp.where((source_of == order[0]) | (receiver == order[0]) | (tallies[receiver] == 0), 0, jnp.maximum(slack, 0))
    moved = jax.random.randint(jax.random.fold_in(own, 4), (number_of // 2,), 0, 1 << 20) % (slack + 1)
    tallies = tallies.at[source_of].add(-moved).at[receiver].add(moved)
    items = jnp.searchsorted(jnp.cumsum(tallies), jnp.arange(rows * top), side="right").astype(jnp.int32)
    listing = items.reshape(top, rows).T
    listing = listing[jax.random.permutation(jax.random.fold_in(own, 1), rows)]
    offset_by = jax.random.randint(jax.random.fold_in(own, 2), (rows, 1), 0, top)
    return jnp.take_along_axis(listing, (jnp.arange(top)[None, :] + offset_by) % top, axis=1)


def portions_of(number_of, total, bound, lean, full):
    weights = [(1 << 20) // math.isqrt(rank ** lean) + 1 for rank in range(1, number_of + 1)]
    largest = bound if full else min(bound, max(-(-total // number_of), total * weights[0] // sum(weights)))
    least = 1 if total - largest >= number_of - 1 else 0
    holding, spare = [largest] + [least] * (number_of - 1), total - largest - least * (number_of - 1)
    while spare > 0:
        candidates = [i for i in range(1, number_of) if holding[i] < largest] or [i for i in range(1, number_of) if holding[i] < bound]
        whole, remaining = sum([weights[i] for i in candidates]), spare
        for i in candidates:
            addition = min(bound - holding[i], max(1, remaining * weights[i] // whole), spare)
            holding[i] = holding[i] + addition
            spare = spare - addition
    return np.array(holding)


def centred(stream_key, extent, width, reach, shards=(), held_as=jnp.bfloat16):
    factor_of = block_levels(stream_key, extent, shards, -0.22, 0.18) if shards else 1.0
    array = jax.random.normal(stream_key, extent, jnp.float32) * width * factor_of
    return jnp.minimum(jnp.maximum(array, -reach), reach).astype(held_as)


def setup_inputs(seed: int = 0) -> dict:
    seeds = jax.random.split(jax.random.key(seed), 16)
    tokens_in = centred(seeds[0], (ROWS, LENGTH, D), 1.0, 6.0, ((0, 16), (1, 8)))
    norm_gain = jnp.clip(1.0 + 0.1 * jax.random.normal(seeds[1], (D,), jnp.float32), 0.5, 1.5).astype(jnp.bfloat16)
    w_query = centred(seeds[2], (D, HEADS * HD), D ** -0.5, 0.1875, ((0, 128),))
    w_key = centred(seeds[3], (D, KV * HD), D ** -0.5, 0.1875, ((0, 128),))
    w_value = centred(seeds[4], (D, KV * HD), D ** -0.5, 0.1875, ((0, 128),))
    qk_gain = jnp.clip(1.0 + 0.1 * jax.random.normal(seeds[5], (2 * HD,), jnp.float32), 0.5, 1.5).astype(jnp.bfloat16)
    w_out = centred(seeds[6], (HEADS * HD, D), (HEADS * HD // 16) ** -0.5, 0.75, ((0, 128),))
    moe_gain = jnp.clip(1.0 + 0.1 * jax.random.normal(seeds[7], (D,), jnp.float32), 0.5, 1.5).astype(jnp.bfloat16)
    w_router = centred(seeds[8], (D, EXPERTS), (4 * D) ** -0.5, 0.09375, ((0, 128),))
    w_gate = centred(seeds[9], (EXPERTS, D, FF), D ** -0.5, 0.1875, ((0, 16), (1, 8)))
    w_up = centred(seeds[10], (EXPERTS, D, FF), D ** -0.5, 0.1875, ((0, 16), (1, 8)))
    w_down = centred(seeds[11], (EXPERTS, FF, D), (FF // 8) ** -0.5, 0.75, ((0, 16), (1, 8)))
    segment_ids = draw_segment_ids(jax.random.fold_in(seeds[15], 71), 0)
    expert_ids_keys = jax.random.split(jax.random.fold_in(seeds[13], 1), ROWS * LENGTH // S_DEV)
    expert_ids_turns = jax.random.permutation(jax.random.fold_in(seeds[13], 3), ROWS * LENGTH // S_DEV)
    expert_ids = jax.vmap(lambda own, number: deal_out(jax.random.fold_in(seeds[13], 2), own, number, S_DEV, EXPERTS, TOPK, CAP, 1))(expert_ids_keys, expert_ids_turns).reshape((ROWS, LENGTH, TOPK))
    out_grad = centred(seeds[14], (ROWS, LENGTH, D), 1.0, 6.0, ((0, 16), (1, 8)))
    return {"tokens_in": tokens_in, "norm_gain": norm_gain, "w_query": w_query, "w_key": w_key, "w_value": w_value, "qk_gain": qk_gain, "w_out": w_out, "moe_gain": moe_gain, "w_router": w_router, "w_gate": w_gate, "w_up": w_up, "w_down": w_down, "segment_ids": segment_ids, "expert_ids": expert_ids, "out_grad": out_grad}


highest = lax.Precision.HIGHEST
epsilon = 1e-06
rope_base = 10000.0

@jax.custom_vjp
def low(v):
    return lax.optimization_barrier(v.astype(jnp.bfloat16)).astype(jnp.float32)

@jax.custom_vjp
def low_back(v):
    return v

def low_keep(v):
    return (low(v), None)

def low_pass(kept, grad):
    return (grad,)

def back_keep(v):
    return (v, None)

def back_low(kept, grad):
    return (low(grad),)
low.defvjp(low_keep, low_pass)
low_back.defvjp(back_keep, back_low)

def rms_norm(values, gain_vec):
    return values * lax.rsqrt(lax.optimization_barrier(jnp.mean(values * values, axis=-1, keepdims=True)) + epsilon) * gain_vec

def rotary(values, positions):
    half_width = values.shape[-1] // 2
    frequency = rope_base ** (-jnp.arange(half_width, dtype=jnp.float32) / half_width)
    angles = positions.astype(jnp.float32)[:, None] * frequency[None, :]
    cosine_table = jnp.cos(angles)[:, None, :]
    sine_table = jnp.sin(angles)[:, None, :]
    first_half = values[..., :half_width]
    second_half = values[..., half_width:]
    return jnp.concatenate([first_half * cosine_table - second_half * sine_table, second_half * cosine_table + first_half * sine_table], axis=-1)

def row_attention(pieces):
    query_row, key_row, value_row, segment_row = pieces
    group_size = HEADS // KV
    query_four = query_row.reshape(LENGTH, KV, group_size, HD)
    scores = low_back(jnp.einsum('skgd,lkd->kgsl', query_four, key_row, precision=highest) * HD ** (-0.5))
    places = jnp.arange(LENGTH, dtype=jnp.int32)
    allowed = (segment_row[None, :] == segment_row[:, None]) & (places[None, :] <= places[:, None])
    scores = jnp.where(allowed, scores, -1000000000.0)
    top_score = lax.optimization_barrier(jnp.max(scores, axis=-1, keepdims=True))
    exp_scores = jnp.exp(scores - top_score)
    soft_prob = exp_scores / lax.optimization_barrier(jnp.sum(exp_scores, axis=-1, keepdims=True))
    attended = jnp.einsum('kgsl,lkd->skgd', low(soft_prob), value_row, precision=highest)
    return attended.reshape(LENGTH, HEADS * HD)

def route_table(routes, row_count):
    blocks = row_count * N_SEQ
    flat_routes = routes.reshape(blocks, S_DEV * TOPK)
    onehot = (flat_routes[..., None] == jnp.arange(EXPERTS, dtype=jnp.int32)).astype(jnp.int32)
    earlier = jnp.cumsum(onehot, axis=1) - onehot
    slot_rank = lax.optimization_barrier(jnp.sum(earlier * onehot, axis=-1))
    slot_index = jnp.arange(blocks, dtype=jnp.int32)[:, None] * CAP + slot_rank
    token_index = jnp.arange(blocks * S_DEV * TOPK, dtype=jnp.int32).reshape(blocks, S_DEV * TOPK) // TOPK
    slot_table = jnp.full((EXPERTS, blocks * CAP), blocks * S_DEV, jnp.int32)
    slot_table = slot_table.at[flat_routes.reshape(-1), slot_index.reshape(-1)].set(token_index.reshape(-1))
    where_at = flat_routes * (blocks * CAP) + slot_index
    return (slot_table, where_at.reshape(-1))

def experts_apply(normed_two, gate_probs, routes, w_gate, w_up, w_down):
    row_count = normed_two.shape[0]
    slot_table, where_at = route_table(routes, row_count)
    flat_rows = normed_two.reshape(-1, D)
    padded = jnp.concatenate([flat_rows, jnp.zeros((1, D), flat_rows.dtype)], axis=0)

    def one_expert(pieces):
        index_row, gate_w, up_w, down_w = pieces
        rows_in = low_back(padded[index_row])
        gate_pre = low_back(jnp.dot(rows_in, gate_w, precision=highest, preferred_element_type=jnp.float32))
        up_pre = low_back(jnp.dot(rows_in, up_w, precision=highest, preferred_element_type=jnp.float32))
        hidden = low(jax.nn.silu(gate_pre) * up_pre)
        return low(low_back(jnp.dot(hidden, down_w, precision=highest, preferred_element_type=jnp.float32)))
    expert_rows = lax.map(jax.checkpoint(one_expert), (slot_table, w_gate, w_up, w_down))
    picked = expert_rows.reshape(-1, D)[where_at].reshape(-1, TOPK, D)
    summed = jnp.einsum('tk,tkd->td', gate_probs.reshape(-1, TOPK), picked, precision=highest)
    return summed.reshape(normed_two.shape)

def block_layer(tokens, norm_gain, w_query, w_key, w_value, qk_gain, w_out, moe_gain, w_router, w_gate, w_up, w_down, segment, routes):
    row_count = tokens.shape[0]
    positions = jnp.arange(LENGTH, dtype=jnp.int32)
    normed_one = low(rms_norm(tokens, norm_gain))
    query_proj = low_back(jnp.einsum('rld,de->rle', normed_one, w_query, precision=highest))
    key_proj = low_back(jnp.einsum('rld,de->rle', normed_one, w_key, precision=highest))
    value_proj = low_back(jnp.einsum('rld,de->rle', normed_one, w_value, precision=highest))
    query_heads = rms_norm(query_proj.reshape(row_count, LENGTH, HEADS, HD), qk_gain[:HD])
    key_heads = rms_norm(key_proj.reshape(row_count, LENGTH, KV, HD), qk_gain[HD:])
    query_rot = low(rotary(query_heads, positions))
    key_rot = low(rotary(key_heads, positions))
    value_low = low(value_proj.reshape(row_count, LENGTH, KV, HD))
    attended = lax.map(jax.checkpoint(row_attention), (query_rot, key_rot, value_low, segment))
    attended = low(low_back(attended))
    attn_mixed = low_back(jnp.einsum('rle,ed->rld', attended, w_out, precision=highest))
    middle = tokens + attn_mixed
    normed_two = low(rms_norm(middle, moe_gain))
    logits = low_back(jnp.einsum('rld,de->rle', normed_two, w_router, precision=highest))
    choose = (routes[..., None] == jnp.arange(EXPERTS, dtype=jnp.int32)).astype(logits.dtype)
    chosen = lax.optimization_barrier(jnp.sum(choose * logits[:, :, None, :], axis=-1))
    gate_probs = jax.nn.softmax(chosen, axis=-1)
    return middle + experts_apply(normed_two, gate_probs, routes, w_gate, w_up, w_down)

def reference(tokens_in, norm_gain, w_query, w_key, w_value, qk_gain, w_out, moe_gain, w_router, w_gate, w_up, w_down, segment_ids, expert_ids, out_grad):
    weights = tuple((tensor.astype(jnp.float32) for tensor in (norm_gain, w_query, w_key, w_value, qk_gain, w_out, moe_gain, w_router, w_gate, w_up, w_down)))
    group_rows = math.gcd(ROWS, max(1, 4096 // LENGTH))
    group_count = ROWS // group_rows

    def regroup(tensor):
        return tensor.reshape((group_count, group_rows) + tensor.shape[1:])

    def group_step(running, pieces):
        tokens_group, segment_group, route_group, cotangent_group = pieces

        def forward(tokens_value, *params):
            return block_layer(tokens_value, *params, segment_group, route_group)
        result, pullback = jax.vjp(forward, tokens_group, *weights)
        gradients = pullback(cotangent_group)
        updated = tuple((before + addend for before, addend in zip(running, gradients[1:])))
        return (updated, (result, gradients[0]))
    zero_grads = tuple((jnp.zeros(tensor.shape, jnp.float32) for tensor in weights))
    summed, (results, input_grads) = lax.scan(group_step, zero_grads, (regroup(tokens_in.astype(jnp.float32)), regroup(segment_ids), regroup(expert_ids), regroup(out_grad.astype(jnp.float32))))
    layer_out = results.reshape(ROWS, LENGTH, D).astype(jnp.bfloat16)
    tokens_grad = input_grads.reshape(ROWS, LENGTH, D).astype(jnp.bfloat16)
    return (layer_out, tokens_grad, summed[0], summed[1], summed[2], summed[3], summed[4], summed[5], summed[6], summed[7], summed[8], summed[9], summed[10])
```

```python
import jax
import jax.numpy as jnp
from jax import lax
from jax.experimental import pallas as pl
from jax.experimental.pallas import tpu as pltpu
from jax.sharding import PartitionSpec as P

KV = 8
HD = 64
TOPK = 8
VMEM_LIMIT = 60 * 2**20

epsilon = 1e-06
rope_base = 10000.0


class Spot:
    def __init__(self):
        row, seq = lax.axis_index("row"), lax.axis_index("seq")
        self.row, self.seq = row, seq
        self.z = lax.div(row, 4)
        self.xl = lax.rem(lax.div(row, 2), 2)
        self.core = lax.rem(row, 2)
        self.y = lax.div(seq, 2)
        self.xh = lax.rem(seq, 2)

    def by_row(self, z, xl):
        return ((z * 2 + xl) * 2 + self.core, self.seq)

    def by_seq(self, y, xh):
        return (self.row, y * 2 + xh)

    def sibling(self):
        return (self.row + 1 - 2 * self.core, self.seq)


def ring(r):
    return lax.rem(r + 1, 4), lax.rem(r + 3, 4), lax.rem(r + 2, 4)


def meet(spot, row=False, seq=False, core=False):
    barrier = pltpu.get_barrier_semaphore()
    partners = []
    if row:
        right, left, _ = ring(spot.z)
        partners += [spot.by_row(right, spot.xl), spot.by_row(left, spot.xl)]
        partners += [spot.by_row(spot.z, 1 - spot.xl)]
    if seq:
        right, left, _ = ring(spot.y)
        partners += [spot.by_seq(right, spot.xh), spot.by_seq(left, spot.xh)]
        partners += [spot.by_seq(spot.y, 1 - spot.xh)]
    if core:
        partners += [spot.sibling()]
    for partner in partners:
        pl.semaphore_signal(
            barrier, inc=1, device_id=partner, device_id_type=pl.DeviceIdType.MESH
        )
    pl.semaphore_wait(barrier, len(partners))


class Wire:
    def __init__(self, spot, send, recv, local):
        self.spot, self.send_sems, self.recv_sems, self.local_sems = spot, send, recv, local
        self.count, self.locals = 0, 0
        self.sent, self.kept = [], []

    def send(self, src, dst, device):
        k = self.count
        self.count += 1
        copy = pltpu.make_async_remote_copy(
            src_ref=src,
            dst_ref=dst,
            send_sem=self.send_sems.at[k],
            recv_sem=self.recv_sems.at[k],
            device_id=device,
            device_id_type=pl.DeviceIdType.MESH,
        )
        copy.start()
        self.sent.append(copy)
        return k

    def wait(self, k, landed):
        pltpu.make_async_remote_copy(
            src_ref=landed,
            dst_ref=landed,
            send_sem=self.send_sems.at[k],
            recv_sem=self.recv_sems.at[k],
            device_id=self.spot.sibling(),
            device_id_type=pl.DeviceIdType.MESH,
        ).wait_recv()

    def keep(self, src, dst):
        copy = pltpu.make_async_copy(src, dst, self.local_sems.at[self.locals])
        self.locals += 1
        copy.start()
        return copy

    def drain(self):
        for copy in self.sent:
            copy.wait_send()


def run(steps):
    steps = list(steps)
    while steps:
        left = []
        for step in steps:
            try:
                next(step)
                left.append(step)
            except StopIteration:
                pass
        steps = left


def gather(wire, own, slot, halves, r, p, dev, sibling=None, other=None, placed=False):
    right, left, opp = ring(r)
    paired = p is not None
    q = 1 - p if paired else None
    passed = []

    def arrive(a, b):
        if sibling is not None:
            here = slot(a, b)
            passed.append((wire.send(here, here, sibling), other(a, b)))

    mine = slot(r, p)
    if paired:
        pair = wire.send(own, mine, dev(r, q))
    to_right = wire.send(own, mine, dev(right, p))
    to_left = wire.send(own, mine, dev(left, p))
    if sibling is not None:
        passed.append((wire.send(own, mine, sibling), other(r, p)))
    stay = None if placed else wire.keep(own, mine)
    yield
    ends = []
    for column in (p, q) if paired else (p,):
        if column is not p:
            wire.wait(pair, slot(r, q))
            to_right = wire.send(slot(r, q), slot(r, q), dev(right, p))
            to_left = wire.send(slot(r, q), slot(r, q), dev(left, p))
            arrive(r, q)
            yield
        wire.wait(to_right, slot(left, column))
        first = halves(slot(left, column))[0]
        end = [(wire.send(first, first, dev(right, p)), halves(slot(opp, column))[0])]
        arrive(left, column)
        wire.wait(to_left, slot(right, column))
        second = halves(slot(right, column))[1]
        if second is not None:
            end.append((wire.send(second, second, dev(left, p)), halves(slot(opp, column))[1]))
        arrive(right, column)
        ends.append((column, end))
        yield
    for column, end in ends:
        for k, landed in end:
            wire.wait(k, landed)
        arrive(opp, column)
    yield
    for k, landed in passed:
        wire.wait(k, landed)
    if stay is not None:
        stay.wait()


def add_rows(dst, *srcs, rows=16):
    lead = dst.shape[:-2]
    spots = [()]
    for size in lead:
        spots = [s + (i,) for s in spots for i in range(size)]
    step = min(rows, dst.shape[-2])

    def body(i, carry):
        at = pl.ds(pl.multiple_of(i * step, step), step)
        for spot in spots:
            total = dst[spot + (at,)].astype(jnp.float32)
            for src in srcs:
                total = total + src[spot + (at,)].astype(jnp.float32)
            dst[spot + (at,)] = total.astype(dst.dtype)
        return carry

    lax.fori_loop(0, dst.shape[-2] // step, body, 0)


def reduce_ring(wire, acc, r, p, dev, buffers, halves, final):
    right, left, opp = ring(r)
    paired = p is not None
    first_half, second_half, from_left, from_right, from_pair = buffers
    columns = (1 - p, p) if paired else (None,)
    moves = []
    for n, column in enumerate(columns):
        a, b = halves(acc(opp, column))
        moves.append(
            (
                wire.send(a, first_half.at[n], dev(right, p)),
                wire.send(b, second_half.at[n], dev(left, p)),
            )
        )
    yield
    steps = []
    for n, column in enumerate(columns):
        wire.wait(moves[n][0], first_half.at[n])
        add_rows(halves(acc(right, column))[0], first_half.at[n])
        k_right = wire.send(acc(right, column), from_left.at[n], dev(right, p))
        wire.wait(moves[n][1], second_half.at[n])
        add_rows(halves(acc(left, column))[1], second_half.at[n])
        k_left = wire.send(acc(left, column), from_right.at[n], dev(left, p))
        steps.append((k_right, k_left))
        yield
    for n, column in enumerate(columns):
        wire.wait(steps[n][0], from_left.at[n])
        wire.wait(steps[n][1], from_right.at[n])
        add_rows(acc(r, column), from_left.at[n], from_right.at[n])
        if paired and n == 0:
            k_pair = wire.send(acc(r, column), from_pair, dev(r, column))
        yield
    if paired:
        wire.wait(k_pair, from_pair)
        final(acc(r, p), from_pair)
    else:
        final(acc(r, None))


def set_sum(out, first, second, rows=16):
    lead = out.shape[:-2]
    spots = [()]
    for size in lead:
        spots = [s + (i,) for s in spots for i in range(size)]
    step = min(rows, out.shape[-2])

    def body(i, carry):
        at = pl.ds(pl.multiple_of(i * step, step), step)
        for spot in spots:
            total = first[spot + (at,)].astype(jnp.float32) + second[spot + (at,)].astype(
                jnp.float32
            )
            out[spot + (at,)] = total.astype(out.dtype)
        return carry

    lax.fori_loop(0, out.shape[-2] // step, body, 0)


def ring_buffers(block, halves, columns, dtype):
    return [
        pltpu.VMEM((columns,) + halves[0], dtype),
        pltpu.VMEM((columns,) + halves[1], dtype),
        pltpu.VMEM((columns,) + block, dtype),
        pltpu.VMEM((columns,) + block, dtype),
        pltpu.VMEM(block, dtype),
    ]


def sems(remote, local):
    return [
        pltpu.SemaphoreType.DMA((remote,)),
        pltpu.SemaphoreType.DMA((remote,)),
        pltpu.SemaphoreType.DMA((local,)),
    ]


def comm_call(kernel, collective_id, outs, in_specs, out_specs, scratch, *args):
    return pl.pallas_call(
        kernel,
        out_shape=outs,
        in_specs=in_specs,
        out_specs=out_specs,
        scratch_shapes=scratch,
        compiler_params=pltpu.CompilerParams(
            collective_id=collective_id, has_side_effects=True, vmem_limit_bytes=VMEM_LIMIT
        ),
    )(*args)


ANY = pl.BlockSpec(memory_space=pl.ANY)
INSIDE = pl.BlockSpec(memory_space=pltpu.VMEM)


def half_rows(ref):
    middle = ref.shape[-2] // 2
    lead = (slice(None),) * (len(ref.shape) - 2)
    return ref.at[lead + (slice(0, middle),)], ref.at[lead + (slice(middle, None),)]


def half_lead(ref):
    middle = ref.shape[0] // 2
    return ref.at[0:middle], ref.at[middle:]


def half_columns(ref):
    middle = ref.shape[-1] // 256 * 128
    lead = (slice(None),) * (len(ref.shape) - 1)
    return ref.at[lead + (slice(0, middle),)], ref.at[lead + (slice(middle, None),)]


def undivided(ref):
    return ref, None


def gather_inputs(dense_one, dense_two, gate, up, down, grads, ids, segments):
    def kernel(
        one_ref,
        two_ref,
        gate_ref,
        up_ref,
        down_ref,
        grads_ref,
        ids_ref,
        segments_ref,
        one_out,
        two_out,
        gate_out,
        up_out,
        down_out,
        grads_out,
        ids_out,
        segments_out,
        one_got,
        two_got,
        one_pair,
        two_pair,
        send,
        recv,
        local,
    ):
        spot = Spot()
        wire = Wire(spot, send, recv, local)
        meet(spot, row=True, seq=True, core=True)

        def dense(own, got, pair, out):
            k = wire.send(own, got, spot.by_seq(spot.y, 1 - spot.xh))
            yield
            wire.wait(k, got)
            pair[...] = own[...] + got[...]
            here = out.at[spot.z, spot.xl, spot.core]
            yield from gather(
                wire,
                pair,
                lambda y, _: here.at[y],
                half_columns,
                spot.y,
                None,
                lambda y, _: spot.by_seq(y, spot.xh),
            )
            yield from gather(
                wire,
                here,
                lambda z, xl: out.at[z, xl, spot.core],
                half_lead,
                spot.z,
                spot.xl,
                spot.by_row,
                spot.sibling(),
                lambda z, xl: out.at[z, xl, 1 - spot.core],
                placed=True,
            )

        def along_seq(own, slot, halves):
            return gather(wire, own, slot, halves, spot.y, spot.xh, spot.by_seq)

        def along_row(own, out, halves):
            return gather(
                wire,
                own,
                lambda z, xl: out.at[z, xl, spot.core],
                halves,
                spot.z,
                spot.xl,
                spot.by_row,
                spot.sibling(),
                lambda z, xl: out.at[z, xl, 1 - spot.core],
            )

        def band(out, depth):
            def slot(y, xh):
                start = pl.multiple_of((y * 2 + xh) * depth, depth)
                return out.at[:, pl.ds(start, depth), :]

            return slot

        run(
            [
                dense(one_ref, one_got, one_pair, one_out),
                dense(two_ref, two_got, two_pair, two_out),
                along_seq(segments_ref, lambda y, xh: segments_out.at[y, xh], undivided),
                along_row(ids_ref, ids_out, undivided),
                along_seq(gate_ref, band(gate_out, gate_ref.shape[1]), half_lead),
                along_seq(up_ref, band(up_out, up_ref.shape[1]), half_lead),
                along_seq(down_ref, band(down_out, down_ref.shape[1]), half_lead),
                along_row(grads_ref, grads_out, half_rows),
            ]
        )
        wire.drain()

    def over_seq(x):
        return jax.ShapeDtypeStruct((x.shape[0], x.shape[1] * 8, x.shape[2]), x.dtype)

    outs = (
        jax.ShapeDtypeStruct((4, 2, 2, 4) + dense_one.shape, dense_one.dtype),
        jax.ShapeDtypeStruct((4, 2, 2, 4) + dense_two.shape, dense_two.dtype),
        over_seq(gate),
        over_seq(up),
        over_seq(down),
        jax.ShapeDtypeStruct((4, 2, 2) + grads.shape, grads.dtype),
        jax.ShapeDtypeStruct((4, 2, 2) + ids.shape, ids.dtype),
        jax.ShapeDtypeStruct((4, 2) + segments.shape, segments.dtype),
    )
    return comm_call(
        kernel,
        0,
        outs,
        [INSIDE, INSIDE] + [ANY] * 6,
        (ANY,) * 8,
        [
            pltpu.VMEM(dense_one.shape, dense_one.dtype),
            pltpu.VMEM(dense_two.shape, dense_two.dtype),
            pltpu.VMEM(dense_one.shape, dense_one.dtype),
            pltpu.VMEM(dense_two.shape, dense_two.dtype),
        ]
        + sems(128, 16),
        dense_one,
        dense_two,
        gate,
        up,
        down,
        grads,
        ids,
        segments,
    )


def gather_keys(own):
    def kernel(own_ref, out, send, recv, local):
        spot = Spot()
        wire = Wire(spot, send, recv, local)
        meet(spot, seq=True)
        run(
            [
                gather(
                    wire,
                    own_ref,
                    lambda y, xh: out.at[y, xh],
                    half_rows,
                    spot.y,
                    spot.xh,
                    spot.by_seq,
                )
            ]
        )
        wire.drain()

    return comm_call(
        kernel,
        1,
        jax.ShapeDtypeStruct((4, 2) + own.shape, own.dtype),
        [ANY],
        ANY,
        sems(16, 2),
        own,
    )


def gather_tokens(own, probs):
    def kernel(own_ref, probs_ref, out, probs_out, send, recv, local):
        spot = Spot()
        wire = Wire(spot, send, recv, local)
        meet(spot, row=True, core=True)

        def along(source, target, halves):
            return gather(
                wire,
                source,
                lambda z, xl: target.at[z, xl, spot.core],
                halves,
                spot.z,
                spot.xl,
                spot.by_row,
                spot.sibling(),
                lambda z, xl: target.at[z, xl, 1 - spot.core],
            )

        run([along(own_ref, out, half_rows), along(probs_ref, probs_out, undivided)])
        wire.drain()

    return comm_call(
        kernel,
        2,
        (
            jax.ShapeDtypeStruct((4, 2, 2) + own.shape, own.dtype),
            jax.ShapeDtypeStruct((4, 2, 2) + probs.shape, probs.dtype),
        ),
        [ANY, ANY],
        (ANY, ANY),
        sems(48, 4),
        own,
        probs,
    )


def core_reduce(wire, spot, terms, acc, got):
    order = []
    right, left, opp = ring(spot.z)
    for z in (opp, right, left, spot.z):
        for xl in (1 - spot.xl, spot.xl):
            order.append((z, xl))
    numbers = [
        wire.send(terms.at[z, xl, 1 - spot.core], got.at[z, xl], spot.sibling()) for z, xl in order
    ]
    stay = wire.keep(terms.at[:, :, spot.core], acc)
    yield
    stay.wait()
    for k, (z, xl) in zip(numbers, order):
        wire.wait(k, got.at[z, xl])
        add_rows(acc.at[z, xl], got.at[z, xl])
        yield


def scatter_tokens(outs, rows, grads):
    def kernel(*refs):
        terms, results, rest = refs[:3], refs[3:6], list(refs[6:])
        send, recv, local = rest[-3:]
        spot = Spot()
        wire = Wire(spot, send, recv, local)
        meet(spot, row=True, core=True)

        def one(term, result, acc, got, buffers, halves):
            yield from core_reduce(wire, spot, term, acc, got)
            yield from reduce_ring(
                wire,
                lambda z, xl: acc.at[z, xl],
                spot.z,
                spot.xl,
                spot.by_row,
                buffers,
                halves,
                lambda a, b: set_sum(result, a, b),
            )

        run(
            [
                one(terms[n], results[n], rest[7 * n], rest[7 * n + 1], rest[7 * n + 2 : 7 * n + 7], half_rows)
                for n in range(3)
            ]
        )
        wire.drain()

    scratch = []
    for array in (rows, outs, grads):
        block = array.shape[3:]
        half = (block[0] // 2, block[1])
        scratch += [
            pltpu.VMEM((4, 2) + block, array.dtype),
            pltpu.VMEM((4, 2) + block, array.dtype),
        ]
        scratch += ring_buffers(block, (half, half), 2, array.dtype)
    row_sum, out_sum, grad_sum = comm_call(
        kernel,
        3,
        tuple(jax.ShapeDtypeStruct(a.shape[3:], jnp.float32) for a in (rows, outs, grads)),
        [ANY] * 3,
        (INSIDE,) * 3,
        scratch + sems(64, 4),
        rows,
        outs,
        grads,
    )
    return out_sum, row_sum, grad_sum


def scatter_keys(terms):
    def kernel(terms_ref, result, acc, *rest):
        send, recv, local = rest[-3:]
        spot = Spot()
        wire = Wire(spot, send, recv, local)
        meet(spot, seq=True)
        wire.keep(terms_ref, acc).wait()
        run(
            [
                reduce_ring(
                    wire,
                    lambda y, xh: acc.at[y, xh],
                    spot.y,
                    spot.xh,
                    spot.by_seq,
                    rest[:5],
                    half_rows,
                    lambda a, b: set_sum(result, a, b),
                )
            ]
        )
        wire.drain()

    block = terms.shape[2:]
    half = (block[0] // 2, block[1])
    return comm_call(
        kernel,
        4,
        jax.ShapeDtypeStruct(block, jnp.float32),
        [ANY],
        INSIDE,
        [pltpu.VMEM(terms.shape, terms.dtype)]
        + ring_buffers(block, (half, half), 2, terms.dtype)
        + sems(16, 2),
        terms,
    )


def scatter_weights(one, two, gate, up, down):
    dense, experts = (one, two), (gate, up, down)

    def kernel(*refs):
        terms, results, rest = refs[:5], refs[5:10], list(refs[10:])
        send, recv, local = rest[-3:]
        spot = Spot()
        wire = Wire(spot, send, recv, local)
        meet(spot, row=True, seq=True, core=True)

        def take(count):
            taken = rest[:count]
            del rest[:count]
            return taken

        def over_all(term, result, acc, got, buffers, more):
            def close(first, second):
                add_rows(first, second)

            yield from core_reduce(wire, spot, term, acc, got)
            yield from reduce_ring(
                wire,
                lambda z, xl: acc.at[z, xl],
                spot.z,
                spot.xl,
                spot.by_row,
                buffers,
                half_lead,
                close,
            )
            mine = acc.at[spot.z, spot.xl]
            yield from reduce_ring(
                wire,
                lambda y, _: mine.at[y],
                spot.y,
                None,
                lambda y, _: spot.by_seq(y, spot.xh),
                more,
                half_columns,
                lambda total: None,
            )
            k = wire.send(mine.at[spot.y], more[4], spot.by_seq(spot.y, 1 - spot.xh))
            yield
            wire.wait(k, more[4])
            set_sum(result, mine.at[spot.y], more[4])

        def over_seq(term, result, acc, buffers):
            depth = term.shape[1] // 8
            stays = [
                wire.keep(term.at[:, n * depth : (n + 1) * depth, :], acc.at[n // 2, n % 2])
                for n in range(8)
            ]
            yield
            for stay in stays:
                stay.wait()
            yield from reduce_ring(
                wire,
                lambda y, xh: acc.at[y, xh],
                spot.y,
                spot.xh,
                spot.by_seq,
                buffers,
                half_lead,
                lambda a, b: set_sum(result, a, b),
            )

        steps = []
        for n in range(2):
            acc, got = take(2)
            steps.append(over_all(terms[n], results[n], acc, got, take(5), take(5)))
        for n in range(2, 5):
            (acc,) = take(1)
            steps.append(over_seq(terms[n], results[n], acc, take(5)))
        run(steps)
        wire.drain()

    scratch, outs = [], []
    for array in dense:
        block = array.shape[3:]
        small = block[1:]
        cut = small[1] // 256 * 128
        half = (block[0] // 2,) + small
        scratch += [pltpu.VMEM((4, 2) + block, array.dtype)] * 2
        scratch += ring_buffers(block, (half, half), 2, array.dtype)
        scratch += ring_buffers(
            small, ((small[0], cut), (small[0], small[1] - cut)), 1, array.dtype
        )
        outs.append(jax.ShapeDtypeStruct(small, jnp.float32))
    for array in experts:
        block = (array.shape[0], array.shape[1] // 8, array.shape[2])
        half = (block[0] // 2,) + block[1:]
        scratch += [pltpu.VMEM((4, 2) + block, array.dtype)]
        scratch += ring_buffers(block, (half, half), 2, array.dtype)
        outs.append(jax.ShapeDtypeStruct(block, jnp.float32))
    return comm_call(
        kernel,
        5,
        tuple(outs),
        [ANY] * 5,
        (INSIDE,) * 5,
        scratch + sems(96, 40),
        one,
        two,
        gate,
        up,
        down,
    )


def rms_norm(values, gain_vec):
    return (
        values * lax.rsqrt(jnp.mean(values * values, axis=-1, keepdims=True) + epsilon) * gain_vec
    )


def rotary(values, positions):
    half_width = values.shape[-1] // 2
    frequency = rope_base ** (-jnp.arange(half_width, dtype=jnp.float32) / half_width)
    angles = positions.astype(jnp.float32)[:, None] * frequency[None, :]
    cosine_table = jnp.cos(angles)[:, None, :]
    sine_table = jnp.sin(angles)[:, None, :]
    first_half = values[..., :half_width]
    second_half = values[..., half_width:]
    return jnp.concatenate(
        [
            first_half * cosine_table - second_half * sine_table,
            second_half * cosine_table + first_half * sine_table,
        ],
        axis=-1,
    )


def head_norms(query_proj, key_proj, qk_full, positions):
    seq_len = query_proj.shape[0]
    query_heads = rms_norm(query_proj.reshape(seq_len, -1, HD), qk_full[:HD])
    key_heads = rms_norm(key_proj.reshape(seq_len, -1, HD), qk_full[HD:])
    return (
        rotary(query_heads, positions).reshape(seq_len, -1),
        rotary(key_heads, positions).reshape(seq_len, -1),
    )


def to_blocks(tensor, pair_count):
    length, columns = tensor.shape
    return tensor.reshape(length, pair_count, columns // pair_count).transpose(1, 0, 2)


def from_blocks(tensor):
    pair_count, length, columns = tensor.shape
    return tensor.transpose(1, 0, 2).reshape(length, pair_count * columns)


def masked_scores(query_block, key_block, allowed):
    group_size = query_block.shape[-1] // key_block.shape[-1]
    query_four = query_block.reshape(query_block.shape[0], 2, group_size, HD)
    key_two = key_block.reshape(key_block.shape[0], 2, HD)
    raw_scores = jnp.einsum(
        "skgd,lkd->kgsl", query_four, key_two, preferred_element_type=jnp.float32
    ) * HD ** (-0.5)
    return (jnp.where(allowed, raw_scores, -1000000000.0), query_four, key_two)


def dot(a, b, dims):
    return lax.dot_general(a, b, (dims, ((), ())), preferred_element_type=jnp.float32)


def shards(
    tokens_in,
    norm_gain,
    w_query,
    w_key,
    w_value,
    qk_gain,
    w_out,
    moe_gain,
    w_router,
    w_gate,
    w_up,
    w_down,
    segment_ids,
    expert_ids,
    out_grad,
):
    _, seq_len, model_width = tokens_in.shape
    seq_count = lax.axis_size("seq")
    row_count = lax.axis_size("row")
    full_len = seq_len * seq_count
    exp_local = w_gate.shape[0]
    expert_count = exp_local * row_count
    capacity = 3 * seq_len * TOPK // (2 * expert_count)
    row_index, seq_index = lax.axis_index("row"), lax.axis_index("seq")
    x_hi = lax.rem(seq_index, 2)
    query_pos = seq_index * seq_len + jnp.arange(seq_len, dtype=jnp.int32)
    key_pos = jnp.arange(full_len, dtype=jnp.int32)
    pair_count = KV // 2
    bf16, f32 = jnp.bfloat16, jnp.float32

    shard_rows = w_query.shape[0]
    extras = jnp.concatenate(
        [
            w_router,
            norm_gain[:, None],
            moe_gain[:, None],
            jnp.pad(qk_gain[:, None], ((0, shard_rows - 1), (0, 0))),
            jnp.zeros((shard_rows, 128 - 3 - expert_count), bf16),
        ],
        axis=1,
    )

    def placed_rows(shard):
        blank = jnp.zeros_like(shard)
        return jnp.where(
            x_hi == 0,
            jnp.concatenate([shard, blank], axis=0),
            jnp.concatenate([blank, shard], axis=0),
        )

    ids_turned = expert_ids[0].T
    segment_rows = jnp.broadcast_to(segment_ids, (8, seq_len))
    dense_one, dense_two, gate_all, up_all, down_all, grads_all, ids_all, segments_all = (
        gather_inputs(
            placed_rows(jnp.concatenate([w_query, w_key, w_value, extras], axis=1)),
            placed_rows(w_out),
            w_gate,
            w_up,
            w_down,
            out_grad[0],
            ids_turned,
            segment_rows,
        )
    )
    proj_width = w_query.shape[1] + w_key.shape[1] + w_value.shape[1]
    query_width = w_query.shape[1]
    key_width = w_key.shape[1]
    dense_one = dense_one.reshape(model_width, -1)
    w_proj = dense_one[:, :proj_width]
    w_out_all = dense_two.reshape(-1, model_width)
    w_router_all = dense_one[:, proj_width : proj_width + expert_count]
    norm_gain_all = dense_one[:, proj_width + expert_count].astype(f32)
    moe_gain_all = dense_one[:, proj_width + expert_count + 1].astype(f32)
    qk_gain_all = dense_one[::shard_rows, proj_width + expert_count + 2].astype(f32)
    grads_all = grads_all.reshape(row_count, seq_len, model_width)
    ids_all = ids_all.reshape(row_count, TOPK, seq_len)
    key_segment = segments_all[:, :, 0].reshape(full_len)

    inputs = tokens_in[0].astype(f32)
    low_one = rms_norm(inputs, norm_gain_all).astype(bf16)
    proj = dot(low_one, w_proj, ((1,), (0,)))
    query_proj = proj[:, :query_width]
    key_proj = proj[:, query_width : query_width + key_width]
    value_proj = proj[:, query_width + key_width :]
    query_rot, key_rot = head_norms(query_proj, key_proj, qk_gain_all, query_pos)
    query_low = query_rot.astype(bf16)
    keys_all = gather_keys(
        jnp.concatenate([key_rot.astype(bf16), value_proj.astype(bf16)], axis=1)
    ).reshape(full_len, -1)
    allowed = (key_segment[None, :] == segment_ids[0][:, None]) & (
        key_pos[None, :] <= query_pos[:, None]
    )
    query_blocks = to_blocks(query_low, pair_count)
    key_blocks = to_blocks(keys_all[:, :key_width], pair_count)
    value_blocks = to_blocks(keys_all[:, key_width:], pair_count)

    def attend(pieces):
        query_block, key_block, value_block = pieces
        scores, query_four, key_two = masked_scores(query_block, key_block, allowed)
        top_score = jnp.max(scores, axis=-1, keepdims=True)
        exp_scores = jnp.exp(scores - top_score)
        row_total = jnp.sum(exp_scores, axis=-1, keepdims=True)
        prob_low = (exp_scores / row_total).astype(bf16)
        value_two = value_block.reshape(value_block.shape[0], 2, HD)
        attended = jnp.einsum("kgsl,lkd->skgd", prob_low, value_two, preferred_element_type=f32)
        return (attended.reshape(attended.shape[0], -1), top_score + jnp.log(row_total))

    attended, log_sums = lax.map(attend, (query_blocks, key_blocks, value_blocks))
    attn_low = from_blocks(attended).astype(bf16)
    middle = inputs + dot(attn_low, w_out_all, ((1,), (0,)))
    low_two = rms_norm(middle, moe_gain_all).astype(bf16)
    logits = dot(low_two, w_router_all, ((1,), (0,)))
    choose = (expert_ids[0][..., None] == jnp.arange(expert_count, dtype=jnp.int32)).astype(f32)
    chosen = jnp.sum(choose * logits[:, None, :], axis=-1)
    gate_probs = jax.nn.softmax(chosen, axis=-1)
    tokens_all, probs_all = gather_tokens(low_two, gate_probs.T)
    tokens_all = tokens_all.reshape(row_count, seq_len, model_width)
    probs_all = probs_all.reshape(row_count, TOPK, seq_len)

    earlier = (
        jnp.arange(seq_len, dtype=jnp.int32)[:, None] < jnp.arange(seq_len, dtype=jnp.int32)
    ).astype(bf16)
    out_part = jnp.zeros((row_count, seq_len, model_width), f32)
    row_part = jnp.zeros((row_count, seq_len, model_width), f32)
    grad_part = jnp.zeros((row_count, expert_count, seq_len), f32)
    gate_wgrad, up_wgrad, down_wgrad = [], [], []
    for expert_slot in range(exp_local):
        expert = row_index * exp_local + expert_slot
        hit = ids_all == expert
        used = jnp.any(hit, axis=1)
        prob = jnp.sum(jnp.where(hit, probs_all, 0.0), axis=1)
        rank = dot(used.astype(bf16), earlier, ((1,), (0,)))
        pick = used[:, None, :] & (
            rank[:, None, :] == jnp.arange(capacity, dtype=f32)[None, :, None]
        )
        pick_low = pick.astype(bf16)
        slot_prob = jnp.sum(jnp.where(pick, prob[:, None, :], 0.0), axis=-1).reshape(-1, 1)
        rows_in = (
            jnp.einsum("rst,rtd->rsd", pick_low, tokens_all, preferred_element_type=f32)
            .astype(bf16)
            .reshape(-1, model_width)
        )
        grad_in = (
            jnp.einsum("rst,rtd->rsd", pick_low, grads_all, preferred_element_type=f32)
            .astype(bf16)
            .reshape(-1, model_width)
        )
        gate_pre = dot(rows_in, gate_all[expert_slot], ((1,), (0,)))
        up_pre = dot(rows_in, up_all[expert_slot], ((1,), (0,)))
        hidden = (jax.nn.silu(gate_pre) * up_pre).astype(bf16)
        expert_rows = dot(hidden, down_all[expert_slot], ((1,), (0,))).astype(bf16).astype(f32)
        grad_wide = grad_in.astype(f32)
        gate_grad = jnp.sum(grad_wide * expert_rows, axis=-1).reshape(row_count, capacity, 1)
        slot_grad = (slot_prob * grad_wide).astype(bf16)
        hidden_grad = dot(slot_grad, down_all[expert_slot], ((1,), (1,)))
        _, swiglu_pull = jax.vjp(
            lambda gate_value, up_value: jax.nn.silu(gate_value) * up_value, gate_pre, up_pre
        )
        gate_pgrad, up_pgrad = swiglu_pull(hidden_grad)
        gate_glow = gate_pgrad.astype(bf16)
        up_glow = up_pgrad.astype(bf16)
        gate_wgrad.append(dot(rows_in, gate_glow, ((0,), (0,))).astype(bf16))
        up_wgrad.append(dot(rows_in, up_glow, ((0,), (0,))).astype(bf16))
        down_wgrad.append(dot(hidden, slot_grad, ((0,), (0,))).astype(bf16))
        row_grad = (
            dot(gate_glow, gate_all[expert_slot], ((1,), (1,)))
            + dot(up_glow, up_all[expert_slot], ((1,), (1,)))
        ).astype(bf16)
        weighted = (slot_prob * expert_rows).astype(bf16)
        out_part = out_part + jnp.einsum(
            "rst,rsd->rtd",
            pick_low,
            weighted.reshape(row_count, capacity, model_width),
            preferred_element_type=f32,
        )
        row_part = row_part + jnp.einsum(
            "rst,rsd->rtd",
            pick_low,
            row_grad.reshape(row_count, capacity, model_width),
            preferred_element_type=f32,
        )
        spread = jnp.sum(jnp.where(pick, gate_grad, 0.0), axis=1)
        grad_part = grad_part + jnp.where(
            (jnp.arange(expert_count, dtype=jnp.int32) == expert)[None, :, None],
            spread[:, None, :],
            0.0,
        )
    blocks = (4, 2, 2)
    out_sum, row_sum, grad_sum = scatter_tokens(
        out_part.astype(bf16).reshape(blocks + (seq_len, model_width)),
        row_part.astype(bf16).reshape(blocks + (seq_len, model_width)),
        grad_part.reshape(blocks + (expert_count, seq_len)),
    )
    layer_out = (middle + out_sum).astype(bf16)
    cotangent = out_grad[0].astype(f32)
    probs_wide = jnp.sum(choose * gate_probs[..., None], axis=1)
    grads_wide = grad_sum.T
    logit_grad = (
        probs_wide
        * (grads_wide - jnp.sum(probs_wide * grads_wide, axis=-1, keepdims=True))
    ).astype(bf16)
    low_two_grad = dot(logit_grad, w_router_all, ((1,), (1,))) + row_sum
    router_wgrad = dot(low_two, logit_grad, ((0,), (0,)))
    _, norm_two_pull = jax.vjp(rms_norm, middle, moe_gain_all)
    middle_norm_grad, gain_two_grad = norm_two_pull(low_two_grad)
    middle_grad = cotangent + middle_norm_grad
    mixed_low = middle_grad.astype(bf16)
    out_wgrad = dot(attn_low, mixed_low, ((0,), (0,)))
    attn_grad = dot(mixed_low, w_out_all, ((1,), (1,))).astype(bf16)

    def attend_back(pieces):
        query_block, key_block, value_block, log_sum, dout_block = pieces
        scores, query_four, key_two = masked_scores(query_block, key_block, allowed)
        soft_prob = jnp.exp(scores - log_sum)
        prob_low = soft_prob.astype(bf16)
        value_two = value_block.reshape(value_block.shape[0], 2, HD)
        dout_four = dout_block.reshape(query_four.shape)
        prob_grad = jnp.einsum("skgd,lkd->kgsl", dout_four, value_two, preferred_element_type=f32)
        score_grad = soft_prob * (
            prob_grad - jnp.sum(soft_prob * prob_grad, axis=-1, keepdims=True)
        )
        score_low = score_grad.astype(bf16)
        scale = HD ** (-0.5)
        query_part = (
            jnp.einsum("kgsl,lkd->skgd", score_low, key_two, preferred_element_type=f32) * scale
        )
        key_part = (
            jnp.einsum("kgsl,skgd->lkd", score_low, query_four, preferred_element_type=f32) * scale
        )
        value_part = jnp.einsum(
            "kgsl,skgd->lkd", prob_low, dout_four, preferred_element_type=f32
        )
        return (
            query_part.reshape(query_part.shape[0], -1),
            key_part.reshape(key_part.shape[0], -1),
            value_part.reshape(value_part.shape[0], -1),
        )

    query_gblocks, key_gblocks, value_gblocks = lax.map(
        attend_back,
        (query_blocks, key_blocks, value_blocks, log_sums, to_blocks(attn_grad, pair_count)),
    )
    key_grads = scatter_keys(
        jnp.concatenate(
            [from_blocks(key_gblocks).astype(bf16), from_blocks(value_gblocks).astype(bf16)],
            axis=1,
        ).reshape(4, 2, seq_len, -1)
    )
    query_grad = from_blocks(query_gblocks)
    _, head_pull = jax.vjp(
        lambda query_in, key_in, gains_in: head_norms(query_in, key_in, gains_in, query_pos),
        query_proj,
        key_proj,
        qk_gain_all,
    )
    query_pgrad, key_pgrad, qk_grad = head_pull((query_grad, key_grads[:, :key_width]))
    proj_glow = jnp.concatenate(
        [query_pgrad.astype(bf16), key_pgrad.astype(bf16), key_grads[:, key_width:].astype(bf16)],
        axis=1,
    )
    proj_wgrad = dot(low_one, proj_glow, ((0,), (0,))).astype(bf16)
    low_one_grad = dot(proj_glow, w_proj, ((1,), (1,)))
    _, norm_one_pull = jax.vjp(rms_norm, inputs, norm_gain_all)
    input_norm_grad, gain_one_grad = norm_one_pull(low_one_grad)
    input_grad = (middle_grad + input_norm_grad).astype(bf16)
    qk_column = jnp.pad(qk_grad[:, None], ((0, 0), (0, shard_rows - 1))).reshape(-1, 1)
    extra_grads = jnp.concatenate(
        [
            router_wgrad,
            gain_one_grad[:, None],
            gain_two_grad[:, None],
            qk_column,
            jnp.zeros((model_width, 128 - 3 - expert_count), f32),
        ],
        axis=1,
    )
    second = jnp.concatenate([out_wgrad, extra_grads], axis=1).astype(bf16)
    dense_blocks = (4, 2, 2, 4, 2 * shard_rows, -1)
    one_sum, two_sum, gate_sum, up_sum, down_sum = scatter_weights(
        proj_wgrad.reshape(dense_blocks),
        second.reshape(dense_blocks),
        jnp.stack(gate_wgrad),
        jnp.stack(up_wgrad),
        jnp.stack(down_wgrad),
    )

    def own_rows(pair):
        return jnp.where(x_hi == 0, pair[:shard_rows], pair[shard_rows:])

    one_own, two_own = own_rows(one_sum), own_rows(two_sum)
    return (
        layer_out[None],
        input_grad[None],
        two_own[:, model_width + expert_count],
        one_own[:, :query_width],
        one_own[:, query_width : query_width + key_width],
        one_own[:, query_width + key_width :],
        two_own[:1, model_width + expert_count + 2],
        two_own[:, :model_width],
        two_own[:, model_width + expert_count + 1],
        two_own[:, model_width : model_width + expert_count],
        gate_sum,
        up_sum,
        down_sum,
    )


def solution(mesh):
    placed = (
        P("row", "seq", None),
        P(("row", "seq")),
        P(("row", "seq"), None),
        P(("row", "seq"), None),
        P(("row", "seq"), None),
        P(("row", "seq")),
        P(("row", "seq"), None),
        P(("row", "seq")),
        P(("row", "seq"), None),
        P("row", "seq", None),
        P("row", "seq", None),
        P("row", "seq", None),
        P("row", "seq"),
        P("row", "seq", None),
        P("row", "seq", None),
    )
    return jax.shard_map(
        shards,
        mesh=mesh,
        in_specs=placed,
        out_specs=(
            P("row", "seq", None),
            P("row", "seq", None),
            P(("row", "seq")),
            P(("row", "seq"), None),
            P(("row", "seq"), None),
            P(("row", "seq"), None),
            P(("row", "seq")),
            P(("row", "seq"), None),
            P(("row", "seq")),
            P(("row", "seq"), None),
            P("row", "seq", None),
            P("row", "seq", None),
            P("row", "seq", None),
        ),
        check_vma=False,
    )
```
